32 devices in a mesh: dp: 4 (over x, core), group: 8 (over z, y).
Axes of the slice: x: 2, y: 2, z: 4, core: 2. Of those that a mesh axis runs over, the one named last changes fastest.
Arguments:
- acts: bfloat16 [512, 2048], P('dp', 'group'), may hold values from -6 to 6
- cotan: bfloat16 [512, 2048], P('dp'), may hold values from -0.375 to 0.375
- stats: float32 [4, 8, 512, 512], P('dp', 'group'), as said below
- roots: bfloat16 [4, 8, 512, 512], P('dp', 'group'), as said below
- owner: int32 [8], replicated, may hold values from 0 to 7, as said below
- task_of: int32 [8], replicated, may hold values from 0 to 7, as said below
- counts: int32 [8], replicated, may hold values from 1 to 2
Outputs:
- update: bfloat16 [2048, 2048], P('dp', 'group')
- new_stats: float32 [4, 8, 512, 512], P('dp', 'group')
- new_roots: bfloat16 [4, 8, 512, 512], P('dp', 'group')
The draws below stay inside these ranges and needn't reach their ends.
Inputs may be any that keep to these rules, and one draw needn't show every extreme that they name: A permutation; owner[t] is the group index of the device that keeps task t's statistic; task t is the left (t even) or right (t odd) factor of the block whose columns are held by group indices t - t % 2 and t - t % 2 + 1. `task_of`: the inverse permutation of owner. Each stats[k, o] is symmetric positive definite. Each roots[k, t] is symmetric.
All inputs are finite; a program needn't handle non-finite values.
Results may differ from the reference program's by a relative error of at most 0.0055.
The reference program's roundings to bfloat16 on the way (of `gradient`, `factor` and `left_part`) count: a program that leaves them out, or rounds other values in their place, can miss the bound.
Values may be sent and summed in bfloat16 or wider, within the bound.
A program may use at most 128 MiB of HBM per device.

```python
import jax
import jax.numpy as jnp
from jax import lax

B = 512
TOKENS = 512
OUT = 2048
IN = 2048
N_DP = 4
N_GROUP = 8


def routing_tables(key):
    owner = jax.random.permutation(jax.random.fold_in(key, 17), N_GROUP).astype(jnp.int32)
    task_of = jnp.argsort(owner, stable=True).astype(jnp.int32)
    return (owner, task_of)


def draw_owner(key, part):
    return routing_tables(key)[0]


def draw_task_of(key, part):
    return routing_tables(key)[1]


def draw_stats(key, part):
    slots = N_DP * N_GROUP
    slot_keys = jax.random.split(jax.random.fold_in(key, 35), slots)
    ranking = jax.vmap(lambda each: jax.random.permutation(each, B))(slot_keys)
    ranking = ranking.reshape(N_DP, N_GROUP, B).astype(jnp.float32) + 1.0
    rough = jax.random.uniform(jax.random.fold_in(key, 33), (N_DP, N_GROUP, B), jnp.float32, 0.6, 1.4)
    base = jax.random.normal(jax.random.fold_in(key, 31), (N_DP, N_GROUP, B, B), jnp.float32)
    exponent = 1.3
    level = 0.05
    weights = level * B ** 1.5 * rough * ranking ** (-exponent)
    coupled = jnp.einsum('...ab,...cb->...ac', base, base) / B + 0.5 * jnp.eye(B, dtype=jnp.float32)
    scale_root = jnp.sqrt(weights)
    return scale_root[..., :, None] * coupled * scale_root[..., None, :]


def draw_roots(key, part):
    noise = jax.random.normal(jax.random.fold_in(key, 41), (N_DP, N_GROUP, B, B), jnp.float32)
    symmetric = (noise + jnp.swapaxes(noise, -1, -2)) * (0.5 / (2.0 * B) ** 0.5)
    diagonal = jax.random.uniform(jax.random.fold_in(key, 42), (N_DP, N_GROUP, B), jnp.float32, 0.5, 1.5)
    return (symmetric + diagonal[..., None] * jnp.eye(B, dtype=jnp.float32)).astype(jnp.bfloat16)


def with_ends(array, stream_key, smallest, top_value):
    extent = array.shape
    index_at = [jax.random.randint(jax.random.fold_in(stream_key, axis), (), 0, extent[axis]) for axis in range(len(extent))]
    array = array.at[tuple(index_at)].set(smallest)
    longest = extent.index(max(extent))
    index_at[longest] = (index_at[longest] + 1) % extent[longest]
    return array.at[tuple(index_at)].set(top_value)


def raised(entries, key, source, target, blocks, factor):
    def block_of(dim):
        return (jnp.arange(entries.shape[dim]) // (entries.shape[dim] // blocks)).reshape((-1,) + (1,) * (entries.ndim - 1 - dim))

    near = jax.random.permutation(key, blocks)[block_of(target)]
    far = (block_of(target) + blocks // 2) % blocks
    return jnp.where((block_of(source) == near) | (block_of(source) == far), factor * entries, entries)


def levels(key, dims, shards, low, top_value):
    def one(dim, parts):
        heights = jax.random.uniform(jax.random.fold_in(jax.random.fold_in(key, 6), dim), (parts,), jnp.float32, low / len(shards), top_value / len(shards))
        return jnp.repeat(jnp.exp(heights), dims[dim] // parts).reshape((-1,) + (1,) * (len(dims) - dim - 1))

    gain = one(*shards[0])
    for cut in shards[1:]:
        gain = gain * one(*cut)
    return gain


def centred(stream_key, shape, spread, most, cuts=(), kind=jnp.bfloat16):
    result = jax.random.normal(stream_key, shape, jnp.float32) * spread
    if len(cuts) > 0:
        result = levels(stream_key, shape, cuts, -0.22, 0.18) * result
    return jnp.clip(result, min=-most, max=most).astype(kind)


def gaussian_with(rng, shape, width, bound, cuts, heavy, held_as=jnp.bfloat16):
    values = width * jax.random.normal(rng, shape, jnp.float32)
    if cuts:
        values = values * levels(rng, shape, cuts, -0.22, 0.18)
    return jnp.clip(raised(values, jax.random.fold_in(rng, 3), *heavy), -bound, bound).astype(held_as)


def setup_inputs(seed: int = 0) -> dict:
    splits = jax.random.split(jax.random.key(seed), 8)
    acts = centred(splits[0], (TOKENS, IN), 1.0, 6.0, ((0, 4), (1, 8)))
    cotan = gaussian_with(splits[1], (TOKENS, OUT), TOKENS ** -0.5, 0.375, ((0, 4),), (0, 1, 4, 2.0))
    stats = draw_stats(jax.random.fold_in(splits[7], 71), 0)
    roots = draw_roots(jax.random.fold_in(splits[7], 71), 0)
    owner = draw_owner(jax.random.fold_in(splits[7], 71), 0)
    task_of = draw_task_of(jax.random.fold_in(splits[7], 71), 0)
    counts = with_ends(jax.random.randint(splits[6], (N_GROUP,), 1, 3), jax.random.fold_in(splits[6], 1), 1, 2).astype(jnp.int32)
    return dict(acts=acts, cotan=cotan, stats=stats, roots=roots, owner=owner, task_of=task_of, counts=counts)


decay_rate = 0.9
ridge = 0.001
highest = lax.Precision.HIGHEST

def newton_root(statistic, turns):
    identity = jnp.eye(statistic.shape[0], dtype=jnp.float32)
    matrix = statistic + ridge * identity
    frobenius = jnp.sqrt(jnp.sum(matrix * matrix))
    initial_root = identity * frobenius ** (-0.25)
    start_scaled = matrix / frobenius

    def one_turn(index, current_state):
        root_now, scaled = current_state
        step_matrix = (5.0 * identity - scaled) / 4.0
        root_now = jnp.dot(root_now, step_matrix, precision=highest)
        squared = jnp.dot(step_matrix, step_matrix, precision=highest)
        scaled = jnp.dot(squared, jnp.dot(squared, scaled, precision=highest), precision=highest)
        return (root_now, scaled)
    return lax.fori_loop(0, turns, one_turn, (initial_root, start_scaled))[0]

def reference(acts, cotan, stats, roots, owner, task_of, counts):
    gradient = jnp.dot(cotan.T, acts, preferred_element_type=jnp.float32).astype(jnp.bfloat16)
    blocks = gradient.reshape(N_DP, B, N_GROUP // 2, B).transpose(0, 2, 1, 3)
    matched_pairs = roots.reshape(N_DP, N_GROUP // 2, 2, B, B)
    slot_counts = counts[task_of]

    def one_row(row_args):
        row_blocks, row_stats, row_roots = row_args
        left_part = jnp.einsum('jab,jbc->jac', row_roots[:, 0].astype(jnp.float32), row_blocks.astype(jnp.float32)).astype(jnp.bfloat16)
        row_update = jnp.einsum('jab,jbc->jac', left_part.astype(jnp.float32), row_roots[:, 1].astype(jnp.float32)).astype(jnp.bfloat16)
        factors = jnp.stack([row_blocks, jnp.swapaxes(row_blocks, 1, 2)], 1).reshape(N_GROUP, B, B)
        grouped_per_slot = factors[task_of].astype(jnp.float32)
        gram_product = jnp.einsum('yne,yie->yni', grouped_per_slot, grouped_per_slot)
        row_new = decay_rate * row_stats + gram_product
        slot_roots = lax.map(lambda entry: newton_root(entry[0], entry[1]), (row_new, slot_counts))
        return (row_update, row_new, slot_roots[owner].astype(jnp.bfloat16))
    updates, new_stats, new_roots = lax.map(one_row, (blocks, stats, matched_pairs))
    update = updates.transpose(0, 2, 1, 3).reshape(N_DP * B, N_GROUP // 2 * B)
    return (update, new_stats, new_roots)
```

```python
import jax
import jax.numpy as jnp
from jax import lax
from jax.sharding import PartitionSpec as P

decay_rate = 0.9
ridge = 0.001


def swapped(x, axis, distance):
    return lax.ppermute(x, axis, [(i, i ^ 1 << distance) for i in range(lax.axis_size(axis))])


def newton_root(statistic, turns):
    identity = jnp.eye(statistic.shape[0], dtype=jnp.float32)
    matrix = statistic + ridge * identity
    frobenius = jnp.sqrt(jnp.sum(matrix * matrix))
    scaled = matrix / frobenius
    step_matrix = (5.0 * identity - scaled) / 4.0
    low = scaled.astype(jnp.bfloat16)
    square = jnp.dot(low, low, preferred_element_type=jnp.float32)
    rest = ((square - 10.0 * scaled) / 16.0).astype(jnp.bfloat16)
    product = (5.0 * scaled - square) / 4.0
    for _ in range(2):
        product = 1.5625 * product + jnp.dot(
            rest, product.astype(jnp.bfloat16), preferred_element_type=jnp.float32
        )
    second = (5.0 * step_matrix - product) / 4.0
    return jnp.where(turns == 1, step_matrix, second) * frobenius ** (-0.25)


def route_blocks(payload, sources, groups):
    order_size, column_count = payload.shape
    strip_rows = order_size // groups
    spread_out = payload.reshape(groups, strip_rows, column_count)
    middle = lax.all_to_all(spread_out, "group", split_axis=0, concat_axis=0, tiled=True)
    chosen = jnp.concatenate(
        [lax.dynamic_slice_in_dim(middle, sources[0, each], 1, 0) for each in range(groups)], 0
    )[None]
    arrived = lax.all_to_all(chosen, "group", split_axis=1, concat_axis=1, tiled=True)
    return arrived.reshape(sources.shape[0], order_size, column_count)


def per_device(acts, cotan, stats, roots, owner, task_of, counts):
    groups = lax.axis_size("group")
    position = lax.axis_index("group")
    order_size = stats.shape[-1]
    half_cols = acts.shape[1]
    column_half = position % 2
    wanted = lax.all_to_all(cotan, "dp", split_axis=1, concat_axis=0, tiled=True)
    gradient = lax.dot_general(
        wanted,
        lax.all_gather(acts, "dp", axis=0, tiled=True),
        (((0,), (0,)), ((), ())),
        preferred_element_type=jnp.float32,
    ).astype(jnp.bfloat16)
    own_root = roots[0, 0]
    other_half, other_root = swapped((gradient, own_root), "group", 0)
    first_half = jnp.where(column_half == 0, gradient, other_half)
    second_half = jnp.where(column_half == 0, other_half, gradient)
    full_block = jnp.concatenate([first_half, second_half], 1)
    left_root = jnp.where(column_half == 0, own_root, other_root)
    right_root = jnp.where(column_half == 0, other_root, own_root)
    left_part = jnp.dot(left_root, full_block, preferred_element_type=jnp.float32).astype(
        jnp.bfloat16
    )
    right_columns = lax.dynamic_slice_in_dim(right_root, column_half * half_cols, half_cols, 1)
    update = jnp.dot(left_part, right_columns, preferred_element_type=jnp.float32).astype(
        jnp.bfloat16
    )
    my_task = task_of[position]
    factor_own = jnp.where(column_half == 1, full_block.T, full_block)
    factor = route_blocks(factor_own, task_of[None, :], groups)[0]
    gram_product = lax.dot_general(
        factor, factor, (((1,), (1,)), ((), ())), preferred_element_type=jnp.float32
    )
    refreshed_statistic = decay_rate * stats[0, 0] + gram_product
    fresh_root = newton_root(refreshed_statistic, counts[my_task]).astype(jnp.bfloat16)
    returned = route_blocks(fresh_root, owner[None, :], groups)[0]
    return (update, refreshed_statistic[None, None], returned[None, None])


def solution(mesh):
    return jax.shard_map(
        per_device,
        mesh=mesh,
        in_specs=(
            P("dp", "group"),
            P("dp", None),
            P("dp", "group", None, None),
            P("dp", "group", None, None),
            P(),
            P(),
            P(),
        ),
        out_specs=(P("dp", "group"), P("dp", "group", None, None), P("dp", "group", None, None)),
        check_vma=False,
    )
```

```python
import functools

import jax
import jax.numpy as jnp
from jax import lax
from jax.experimental import pallas as pl
from jax.experimental.pallas import tpu as pltpu
from jax.sharding import PartitionSpec as P

decay_rate = 0.9
ridge = 0.001
tile = 128
f32 = jnp.float32
bf16 = jnp.bfloat16


def dot(a, b, over=((1,), (0,))):
    return lax.dot_general(a, b, (over, ((), ())), preferred_element_type=f32)


def newton_root(matrix, turns, identity):
    size = jnp.sqrt(jnp.sum(matrix * matrix, keepdims=True))
    scaled = matrix * (1.0 / size)
    first = 1.25 * identity - 0.25 * scaled
    low = scaled.astype(bf16)
    square = dot(low, low)
    rest = ((square - 10.0 * scaled) * 0.0625).astype(bf16)
    product = 1.25 * scaled - 0.25 * square
    for _ in range(2):
        product = 1.5625 * product + dot(rest, product.astype(bf16))
    second = 1.25 * first - 0.25 * product
    return jnp.where(turns == 1, first, second) * (1.0 / jnp.sqrt(jnp.sqrt(size)))


def kernel(
    groups, dps, blocks,
    owner, task_of, counts, acts, cotan, stats, roots,
    update, new_stats, new_roots,
    acts_all, pairs, cot_all, lows, mid, staged, final, root_pair, block_ref,
    acts_send, acts_recv, pair_send, pair_recv, cot_send, cot_recv,
    one_send, one_recv, two_send, two_recv, root_send, root_recv,
):
    me = lax.axis_index("group")
    row = lax.axis_index("dp")
    order = stats.shape[-1]
    half = acts.shape[1]
    parity = lax.rem(me, 2)
    partner = me + 1 - 2 * parity
    first = me - parity

    def group_at(d):
        return lax.rem(me + d, groups)

    def row_at(d):
        return lax.rem(row + d, dps)

    def copy(src, dst, send, recv, axis, to):
        return pltpu.make_async_remote_copy(
            src_ref=src, dst_ref=dst, send_sem=send, recv_sem=recv,
            device_id={axis: to}, device_id_type=pl.DeviceIdType.MESH,
        )

    barrier = pltpu.get_barrier_semaphore()
    for d in range(1, groups):
        pl.semaphore_signal(barrier, inc=1, device_id={"group": group_at(d)}, device_id_type=pl.DeviceIdType.MESH)
    for d in range(1, dps):
        pl.semaphore_signal(barrier, inc=1, device_id={"dp": row_at(d)}, device_id_type=pl.DeviceIdType.MESH)
    for at, (i, j) in enumerate(blocks):
        part = stats[i * tile : (i + 1) * tile, j * tile : (j + 1) * tile].astype(bf16)
        lows[at * tile : (at + 1) * tile, :] = part
    strip = lows.shape[0] // groups
    pl.semaphore_wait(barrier, groups + dps - 2)

    def strip_of(g):
        return lows.at[pl.ds(pl.multiple_of(g * strip, strip), strip), :]

    act_copies = [
        copy(acts, acts_all.at[me], acts_send.at[d], acts_recv.at[d], "group", group_at(d))
        for d in range(1, groups)
    ]
    cot_copies = []
    for d in range(1, dps):
        to = row_at(d)
        columns = cotan.at[:, pl.ds(pl.multiple_of(to * order, order), order)]
        cot_copies.append(copy(columns, cot_all.at[row], cot_send.at[d], cot_recv.at[d], "dp", to))
    one_copies = [
        copy(strip_of(group_at(d)), mid.at[me], one_send.at[d], one_recv.at[d], "group", group_at(d))
        for d in range(1, groups)
    ]
    root_copy = copy(roots, root_pair.at[parity], root_send.at[0], root_recv.at[0], "group", partner)
    for each in [*act_copies, *one_copies, *cot_copies, root_copy]:
        each.start()

    acts_all[me] = acts[...]
    mid[me] = lows[pl.ds(pl.multiple_of(me * strip, strip), strip), :]
    root_pair[parity] = roots[...]
    cot_all[row] = cotan[:, pl.ds(pl.multiple_of(row * order, order), order)]
    mine = task_of[me]
    task_first = mine - lax.rem(mine, 2)

    def arrived(buffer, back, send, recv, axis, d):
        copy(buffer.at[back], buffer.at[back], send.at[d], recv.at[d], axis, back).wait_recv()

    for d in range(1, groups):
        arrived(acts_all, lax.rem(me + groups - d, groups), acts_send, acts_recv, "group", d)
    for i in range(2):
        pairs[row, i] = acts_all[first + i]
        pairs[row, 2 + i] = acts_all[task_first + i]
    pair_copies = [
        copy(pairs.at[row], pairs.at[row], pair_send.at[d], pair_recv.at[d], "dp", row_at(d))
        for d in range(1, dps)
    ]
    for each in pair_copies:
        each.start()
    for d in range(1, groups):
        arrived(mid, lax.rem(me + groups - d, groups), one_send, one_recv, "group", d)
    two_copies = []
    for d in range(1, groups):
        staged[d] = mid[owner[group_at(d)]]
        each = copy(staged.at[d], final.at[me], two_send.at[d], two_recv.at[d], "group", group_at(d))
        each.start()
        two_copies.append(each)
    final[me] = mid[owner[me]]

    for d in range(1, dps):
        arrived(cot_all, lax.rem(row + dps - d, dps), cot_send, cot_recv, "dp", d)
    tokens = dps * acts.shape[0]
    cot_t = cot_all[...].reshape(tokens, order).T
    for d in range(1, dps):
        arrived(pairs, lax.rem(row + dps - d, dps), pair_send, pair_recv, "dp", d)

    def gradient_into(start):
        for i in range(2):
            part = dot(cot_t, pairs[:, start + i].reshape(tokens, half))
            block_ref[:, i * half : (i + 1) * half] = part.astype(bf16)
        return block_ref[...]

    def gram(block, side):
        return jnp.where(side == 1, dot(block, block, ((0,), (0,))), dot(block, block, ((1,), (1,))))

    new_stats[...] = decay_rate * stats[...] + gram(gradient_into(2), lax.rem(mine, 2))
    own = gradient_into(0)
    own_gram = gram(own, parity)
    copy(roots, root_pair.at[1 - parity], root_send.at[0], root_recv.at[0], "group", partner).wait_recv()
    left_part = dot(root_pair[0], own).astype(bf16)
    right = root_pair[1, :, pl.ds(pl.multiple_of(parity * half, half), half)]
    update[...] = dot(left_part, right).astype(bf16)

    for d in range(1, groups):
        arrived(final, lax.rem(me + groups - d, groups), two_send, two_recv, "group", d)
    packed = final[...].reshape(lows.shape).astype(f32)
    found = {b: packed[at * tile : (at + 1) * tile] for at, b in enumerate(blocks)}
    count = range(order // tile)
    whole = jnp.concatenate(
        [
            jnp.concatenate([found[i, j] if (i, j) in found else found[j, i].T for j in count], 1)
            for i in count
        ],
        0,
    )
    shape = (order, order)
    eye = lax.broadcasted_iota(jnp.int32, shape, 0) == lax.broadcasted_iota(jnp.int32, shape, 1)
    identity = jnp.where(eye, 1.0, 0.0).astype(f32)
    matrix = decay_rate * whole + own_gram + ridge * identity
    new_roots[...] = newton_root(matrix, counts[me], identity).astype(bf16)
    for each in [*act_copies, *one_copies, *cot_copies, root_copy, *pair_copies, *two_copies]:
        each.wait_send()


def per_device(acts, cotan, stats, roots, owner, task_of, counts):
    groups, dps = lax.axis_size("group"), lax.axis_size("dp")
    order, half = stats.shape[-1], acts.shape[1]
    count = range(order // tile)
    blocks = [(i, j) for i in count for j in count if j >= i]
    if len(blocks) * tile % (16 * groups):
        blocks = [(i, j) for i in count for j in count]
    rows = len(blocks) * tile
    strips = pltpu.VMEM((groups, rows // groups, tile), bf16)
    in_vmem, in_smem = (pl.BlockSpec(memory_space=m) for m in (pltpu.VMEM, pltpu.SMEM))
    over_group, over_dp = (pltpu.SemaphoreType.DMA((n,)) for n in (groups, dps))
    update, new_stats, new_roots = pl.pallas_call(
        functools.partial(kernel, groups, dps, blocks),
        out_shape=(
            jax.ShapeDtypeStruct((order, half), bf16),
            jax.ShapeDtypeStruct((order, order), f32),
            jax.ShapeDtypeStruct((order, order), bf16),
        ),
        in_specs=[in_smem] * 3 + [in_vmem] * 4,
        out_specs=(in_vmem,) * 3,
        scratch_shapes=[
            pltpu.VMEM((groups, *acts.shape), bf16),
            pltpu.VMEM((dps, 4, *acts.shape), bf16),
            pltpu.VMEM((dps, acts.shape[0], order), bf16),
            pltpu.VMEM((rows, tile), bf16),
            strips,
            strips,
            strips,
            pltpu.VMEM((2, order, order), bf16),
            pltpu.VMEM((order, order), bf16),
            *[over_group] * 2,
            *[over_dp] * 4,
            *[over_group] * 4,
            *[pltpu.SemaphoreType.DMA((1,))] * 2,
        ],
        compiler_params=pltpu.CompilerParams(
            collective_id=0, has_side_effects=True, vmem_limit_bytes=48 * 2**20
        ),
    )(owner, task_of, counts, acts, cotan, stats[0, 0], roots[0, 0])
    return update, new_stats[None, None], new_roots[None, None]


def solution(mesh):
    return jax.shard_map(
        per_device,
        mesh=mesh,
        in_specs=(
            P("dp", "group"),
            P("dp", None),
            P("dp", "group", None, None),
            P("dp", "group", None, None),
            P(),
            P(),
            P(),
        ),
        out_specs=(P("dp", "group"), P("dp", "group", None, None), P("dp", "group", None, None)),
        check_vma=False,
    )
```

```python
import functools

import jax
import jax.numpy as jnp
from jax import lax
from jax.experimental import pallas as pl
from jax.experimental.pallas import tpu as pltpu
from jax.sharding import PartitionSpec as P

decay_rate = 0.9
ridge = 0.001
tile = 128
f32 = jnp.float32
bf16 = jnp.bfloat16


def dot(a, b, over=((1,), (0,))):
    return lax.dot_general(a, b, (over, ((), ())), preferred_element_type=f32)


def newton_root(matrix, turns, identity):
    size = jnp.sqrt(jnp.sum(matrix * matrix, keepdims=True))
    scaled = matrix * (1.0 / size)
    first = 1.25 * identity - 0.25 * scaled
    low = scaled.astype(bf16)
    square = dot(low, low)
    rest = ((square - 10.0 * scaled) * 0.0625).astype(bf16)
    product = 1.25 * scaled - 0.25 * square
    for _ in range(2):
        product = 1.5625 * product + dot(rest, product.astype(bf16))
    second = 1.25 * first - 0.25 * product
    return jnp.where(turns == 1, first, second) * (1.0 / jnp.sqrt(jnp.sqrt(size)))


def kernel(
    groups, dps, blocks,
    owner, task_of, counts, acts, cotan, stats, roots,
    update, new_stats, new_roots,
    act_mid, act_staged, act_final, pairs, cot_all, lows, mid, staged, final, root_low, root_in, root_pair, block_ref,
    acts_send, acts_recv, pick_send, pick_recv, one_send, one_recv, two_send, two_recv,
    own_send, own_recv, other_send, other_recv, task_send, task_recv, cot_send, cot_recv,
    near_send, near_recv, root_send, root_recv,
):
    me = lax.axis_index("group")
    row = lax.axis_index("dp")
    order = stats.shape[-1]
    half = acts.shape[1]
    parity = lax.rem(me, 2)
    partner = me + 1 - 2 * parity
    first = me - parity

    def group_at(d):
        return lax.rem(me + d, groups)

    def row_at(d):
        return lax.rem(row + d, dps)

    def copy(src, dst, send, recv, axis, to):
        return pltpu.make_async_remote_copy(
            src_ref=src, dst_ref=dst, send_sem=send, recv_sem=recv,
            device_id={axis: to}, device_id_type=pl.DeviceIdType.MESH,
        )

    barrier = pltpu.get_barrier_semaphore()
    for d in range(1, groups):
        pl.semaphore_signal(barrier, inc=1, device_id={"group": group_at(d)}, device_id_type=pl.DeviceIdType.MESH)
    for d in range(1, dps):
        pl.semaphore_signal(barrier, inc=1, device_id={"dp": row_at(d)}, device_id_type=pl.DeviceIdType.MESH)
    for at, (i, j) in enumerate(blocks):
        part = stats[i * tile : (i + 1) * tile, j * tile : (j + 1) * tile].astype(bf16)
        lows[at * tile : (at + 1) * tile, :] = part
        root_low[at * tile : (at + 1) * tile, :] = roots[i * tile : (i + 1) * tile, j * tile : (j + 1) * tile]
    strip = lows.shape[0] // groups
    pl.semaphore_wait(barrier, groups + dps - 2)

    def strip_of(g):
        return lows.at[pl.ds(pl.multiple_of(g * strip, strip), strip), :]

    cut = act_final.shape[1]
    depth = act_final.shape[3]

    def act_strip(g):
        return pl.ds(pl.multiple_of(g * depth, depth), depth) if cut > 1 else slice(None)

    act_copies = [
        copy(acts.at[act_strip(group_at(d)), :], act_mid.at[me], acts_send.at[d], acts_recv.at[d], "group", group_at(d))
        for d in range(1, groups)
    ]
    near_copy = copy(acts, pairs.at[row, parity], near_send.at[0], near_recv.at[0], "group", partner)
    own_copies = [
        copy(acts, pairs.at[row, parity], own_send.at[d], own_recv.at[d], "dp", row_at(d))
        for d in range(1, dps)
    ]
    cot_copies = []
    for d in range(1, dps):
        to = row_at(d)
        columns = cotan.at[:, pl.ds(pl.multiple_of(to * order, order), order)]
        cot_copies.append(copy(columns, cot_all.at[row], cot_send.at[d], cot_recv.at[d], "dp", to))
    one_copies = [
        copy(strip_of(group_at(d)), mid.at[me], one_send.at[d], one_recv.at[d], "group", group_at(d))
        for d in range(1, groups)
    ]
    root_copy = copy(root_low, root_in, root_send.at[0], root_recv.at[0], "group", partner)
    for each in [near_copy, *act_copies, *one_copies, *cot_copies, *own_copies, root_copy]:
        each.start()

    pairs[row, parity] = acts[...]
    act_mid[me] = acts[act_strip(me), :]
    mid[me] = lows[pl.ds(pl.multiple_of(me * strip, strip), strip), :]
    root_pair[parity] = roots[...]
    cot_all[row] = cotan[:, pl.ds(pl.multiple_of(row * order, order), order)]
    mine = task_of[me]

    def back(d):
        return lax.rem(me + groups - d, groups)

    def row_back(d):
        return lax.rem(row + dps - d, dps)

    def arrived(place, send, recv, axis, source):
        copy(place, place, send, recv, axis, source).wait_recv()

    other = pairs.at[row, 1 - parity]
    arrived(other, near_send.at[0], near_recv.at[0], "group", partner)
    other_copies = [
        copy(other, other, other_send.at[d], other_recv.at[d], "dp", row_at(d)) for d in range(1, dps)
    ]
    for each in other_copies:
        each.start()

    for d in range(1, groups):
        arrived(act_mid.at[back(d)], acts_send.at[d], acts_recv.at[d], "group", back(d))
    start = mine - lax.rem(mine, 2)
    pick_copies = []
    if cut > 1:
        for d in range(1, groups):
            task = task_of[group_at(d)]
            base = task - lax.rem(task, 2)
            for i in range(2):
                act_staged[d, i] = act_mid[base + i]
            each = copy(act_staged.at[d], act_final.at[row, me], pick_send.at[d], pick_recv.at[d], "group", group_at(d))
            each.start()
            pick_copies.append(each)
        for i in range(2):
            act_final[row, me, i] = act_mid[start + i]
        for d in range(1, groups):
            arrived(act_final.at[row, back(d)], pick_send.at[d], pick_recv.at[d], "group", back(d))
    else:
        for i in range(2):
            act_final[row, 0, i] = act_mid[start + i]
    task_copies = [
        copy(act_final.at[row], act_final.at[row], task_send.at[d], task_recv.at[d], "dp", row_at(d))
        for d in range(1, dps)
    ]
    for each in task_copies:
        each.start()
    for d in range(1, groups):
        arrived(mid.at[back(d)], one_send.at[d], one_recv.at[d], "group", back(d))
    two_copies = []
    for d in range(1, groups):
        staged[d] = mid[owner[group_at(d)]]
        each = copy(staged.at[d], final.at[me], two_send.at[d], two_recv.at[d], "group", group_at(d))
        each.start()
        two_copies.append(each)
    final[me] = mid[owner[me]]

    for d in range(1, dps):
        arrived(cot_all.at[row_back(d)], cot_send.at[d], cot_recv.at[d], "dp", row_back(d))
    tokens = dps * acts.shape[0]
    cot_t = cot_all[...].reshape(tokens, order).T
    for d in range(1, dps):
        arrived(pairs.at[row_back(d), parity], own_send.at[d], own_recv.at[d], "dp", row_back(d))
        arrived(pairs.at[row_back(d), 1 - parity], other_send.at[d], other_recv.at[d], "dp", row_back(d))

    def gradient_of(halves):
        for i in range(2):
            part = dot(cot_t, halves[i].reshape(tokens, half))
            block_ref[:, i * half : (i + 1) * half] = part.astype(bf16)
        return block_ref[...]

    def gram(block, side):
        return jnp.where(side == 1, dot(block, block, ((0,), (0,))), dot(block, block, ((1,), (1,))))

    def unpacked(packed):
        found = {b: packed[at * tile : (at + 1) * tile] for at, b in enumerate(blocks)}
        count = range(order // tile)
        rows = [[found[i, j] if (i, j) in found else found[j, i].T for j in count] for i in count]
        return jnp.concatenate([jnp.concatenate(each, 1) for each in rows], 0)

    own = gradient_of([pairs[:, i] for i in range(2)])
    own_gram = gram(own, parity)
    arrived(root_in, root_send.at[0], root_recv.at[0], "group", partner)
    root_pair[1 - parity] = unpacked(root_in[...].astype(f32)).astype(bf16)
    left_part = dot(root_pair[0], own).astype(bf16)
    right = root_pair[1, :, pl.ds(pl.multiple_of(parity * half, half), half)]
    update[...] = dot(left_part, right).astype(bf16)

    for d in range(1, dps):
        arrived(act_final.at[row_back(d)], task_send.at[d], task_recv.at[d], "dp", row_back(d))
    task_block = gradient_of([act_final[:, :, i] for i in range(2)])
    new_stats[...] = decay_rate * stats[...] + gram(task_block, lax.rem(mine, 2))

    for d in range(1, groups):
        arrived(final.at[back(d)], two_send.at[d], two_recv.at[d], "group", back(d))
    whole = unpacked(final[...].reshape(lows.shape).astype(f32))
    shape = (order, order)
    eye = lax.broadcasted_iota(jnp.int32, shape, 0) == lax.broadcasted_iota(jnp.int32, shape, 1)
    identity = jnp.where(eye, 1.0, 0.0).astype(f32)
    matrix = decay_rate * whole + own_gram + ridge * identity
    new_roots[...] = newton_root(matrix, counts[me], identity).astype(bf16)
    sent = [near_copy, root_copy, *act_copies, *own_copies, *other_copies, *pick_copies]
    for each in [*sent, *task_copies, *cot_copies, *one_copies, *two_copies]:
        each.wait_send()


def per_device(acts, cotan, stats, roots, owner, task_of, counts):
    groups, dps = lax.axis_size("group"), lax.axis_size("dp")
    order, half = stats.shape[-1], acts.shape[1]
    count = range(order // tile)
    blocks = [(i, j) for i in count for j in count if j >= i]
    if len(blocks) * tile % (16 * groups):
        blocks = [(i, j) for i in count for j in count]
    rows = len(blocks) * tile
    cut = groups if acts.shape[0] % (16 * groups) == 0 else 1
    depth = acts.shape[0] // cut
    strips = pltpu.VMEM((groups, rows // groups, tile), bf16)
    in_vmem, in_smem = (pl.BlockSpec(memory_space=m) for m in (pltpu.VMEM, pltpu.SMEM))
    over_group, over_dp = (pltpu.SemaphoreType.DMA((n,)) for n in (groups, dps))
    update, new_stats, new_roots = pl.pallas_call(
        functools.partial(kernel, groups, dps, blocks),
        out_shape=(
            jax.ShapeDtypeStruct((order, half), bf16),
            jax.ShapeDtypeStruct((order, order), f32),
            jax.ShapeDtypeStruct((order, order), bf16),
        ),
        in_specs=[in_smem] * 3 + [in_vmem] * 4,
        out_specs=(in_vmem,) * 3,
        scratch_shapes=[
            pltpu.VMEM((groups, depth, half), bf16),
            pltpu.VMEM((cut, 2, depth, half), bf16),
            pltpu.VMEM((dps, cut, 2, depth, half), bf16),
            pltpu.VMEM((dps, 2, *acts.shape), bf16),
            pltpu.VMEM((dps, acts.shape[0], order), bf16),
            pltpu.VMEM((rows, tile), bf16),
            strips,
            strips,
            strips,
            pltpu.VMEM((rows, tile), bf16),
            pltpu.VMEM((rows, tile), bf16),
            pltpu.VMEM((2, order, order), bf16),
            pltpu.VMEM((order, order), bf16),
            *[over_group] * 8,
            *[over_dp] * 8,
            *[pltpu.SemaphoreType.DMA((1,))] * 4,
        ],
        compiler_params=pltpu.CompilerParams(
            collective_id=0, has_side_effects=True, vmem_limit_bytes=48 * 2**20
        ),
    )(owner, task_of, counts, acts, cotan, stats[0, 0], roots[0, 0])
    return update, new_stats[None, None], new_roots[None, None]


def solution(mesh):
    return jax.shard_map(
        per_device,
        mesh=mesh,
        in_specs=(
            P("dp", "group"),
            P("dp", None),
            P("dp", "group", None, None),
            P("dp", "group", None, None),
            P(),
            P(),
            P(),
        ),
        out_specs=(P("dp", "group"), P("dp", "group", None, None), P("dp", "group", None, None)),
        check_vma=False,
    )
```

```python
import functools

import jax
import jax.numpy as jnp
from jax import lax
from jax.experimental import pallas as pl
from jax.experimental.pallas import tpu as pltpu
from jax.sharding import PartitionSpec as P

decay_rate = 0.9
ridge = 0.001
tile = 128
f32 = jnp.float32
bf16 = jnp.bfloat16


def dot(a, b, over=((1,), (0,))):
    return lax.dot_general(a, b, (over, ((), ())), preferred_element_type=f32)


def newton_root(matrix, turns, identity):
    size = jnp.sqrt(jnp.sum(matrix * matrix, keepdims=True))
    scaled = matrix * (1.0 / size)
    first = 1.25 * identity - 0.25 * scaled
    low = scaled.astype(bf16)
    square = dot(low, low)
    rest = ((square - 10.0 * scaled) * 0.0625).astype(bf16)
    product = 1.25 * scaled - 0.25 * square
    for _ in range(2):
        product = 1.5625 * product + dot(rest, product.astype(bf16))
    second = 1.25 * first - 0.25 * product
    return jnp.where(turns == 1, first, second) * (1.0 / jnp.sqrt(jnp.sqrt(size)))


def kernel(
    groups, dps, blocks,
    owner, task_of, counts, acts, cotan, stats_in, roots,
    update, new_stats, new_roots,
    act_mid, act_staged, act_final, pairs, cot_all, lows, mid, staged, final, root_low, root_in, root_pair, block_ref, stats,
    acts_send, acts_recv, pick_send, pick_recv, one_send, one_recv, two_send, two_recv,
    own_send, own_recv, other_send, other_recv, task_send, task_recv, cot_send, cot_recv,
    near_send, near_recv, root_send, root_recv, load_sem,
):
    me = lax.axis_index("group")
    row = lax.axis_index("dp")
    order = stats.shape[-1]
    half = acts.shape[1]
    parity = lax.rem(me, 2)
    partner = me + 1 - 2 * parity
    first = me - parity

    def group_at(d):
        return lax.rem(me + d, groups)

    def row_at(d):
        return lax.rem(row + d, dps)

    def copy(src, dst, send, recv, axis, to):
        return pltpu.make_async_remote_copy(
            src_ref=src, dst_ref=dst, send_sem=send, recv_sem=recv,
            device_id={axis: to}, device_id_type=pl.DeviceIdType.MESH,
        )

    barrier = pltpu.get_barrier_semaphore()
    for d in range(1, groups):
        pl.semaphore_signal(barrier, inc=1, device_id={"group": group_at(d)}, device_id_type=pl.DeviceIdType.MESH)
    for d in range(1, dps):
        pl.semaphore_signal(barrier, inc=1, device_id={"dp": row_at(d)}, device_id_type=pl.DeviceIdType.MESH)
    columns = cotan.at[:, pl.ds(pl.multiple_of(row * order, order), order)]
    stats_load, roots_load, acts_load, cotan_load = loads = [
        pltpu.make_async_copy(src, dst, load_sem.at[i])
        for i, (src, dst) in enumerate(
            [
                (stats_in, stats),
                (roots, root_pair.at[parity]),
                (acts, pairs.at[row, parity]),
                (columns, cot_all.at[row]),
            ]
        )
    ]
    for each in loads:
        each.start()
    strip = lows.shape[0] // groups
    pl.semaphore_wait(barrier, groups + dps - 2)

    def strip_of(g):
        return lows.at[pl.ds(pl.multiple_of(g * strip, strip), strip), :]

    cut = act_final.shape[1]
    depth = act_final.shape[3]

    def act_strip(g):
        return pl.ds(pl.multiple_of(g * depth, depth), depth) if cut > 1 else slice(None)

    act_copies = [
        copy(acts.at[act_strip(group_at(d)), :], act_mid.at[me], acts_send.at[d], acts_recv.at[d], "group", group_at(d))
        for d in range(1, groups)
    ]
    near_copy = copy(acts, pairs.at[row, parity], near_send.at[0], near_recv.at[0], "group", partner)
    own_copies = [
        copy(acts, pairs.at[row, parity], own_send.at[d], own_recv.at[d], "dp", row_at(d))
        for d in range(1, dps)
    ]
    cot_copies = []
    for d in range(1, dps):
        to = row_at(d)
        columns = cotan.at[:, pl.ds(pl.multiple_of(to * order, order), order)]
        cot_copies.append(copy(columns, cot_all.at[row], cot_send.at[d], cot_recv.at[d], "dp", to))
    one_copies = [
        copy(strip_of(group_at(d)), mid.at[me], one_send.at[d], one_recv.at[d], "group", group_at(d))
        for d in range(1, groups)
    ]
    root_copy = copy(root_low, root_in, root_send.at[0], root_recv.at[0], "group", partner)
    for each in [near_copy, *act_copies, *cot_copies, *own_copies]:
        each.start()
    stats_load.wait()
    for at, (i, j) in enumerate(blocks):
        part = stats[i * tile : (i + 1) * tile, j * tile : (j + 1) * tile].astype(bf16)
        lows[at * tile : (at + 1) * tile, :] = part
    for each in one_copies:
        each.start()
    mid[me] = lows[pl.ds(pl.multiple_of(me * strip, strip), strip), :]
    roots_load.wait()
    for at, (i, j) in enumerate(blocks):
        part = root_pair[parity, i * tile : (i + 1) * tile, j * tile : (j + 1) * tile]
        root_low[at * tile : (at + 1) * tile, :] = part
    root_copy.start()
    acts_load.wait()
    act_mid[me] = pairs[row, parity, act_strip(me), :]
    cotan_load.wait()
    mine = task_of[me]

    def back(d):
        return lax.rem(me + groups - d, groups)

    def row_back(d):
        return lax.rem(row + dps - d, dps)

    def arrived(place, send, recv, axis, source):
        copy(place, place, send, recv, axis, source).wait_recv()

    other = pairs.at[row, 1 - parity]
    arrived(other, near_send.at[0], near_recv.at[0], "group", partner)
    other_copies = [
        copy(other, other, other_send.at[d], other_recv.at[d], "dp", row_at(d)) for d in range(1, dps)
    ]
    for each in other_copies:
        each.start()

    for d in range(1, groups):
        arrived(act_mid.at[back(d)], acts_send.at[d], acts_recv.at[d], "group", back(d))
    start = mine - lax.rem(mine, 2)
    pick_copies = []
    if cut > 1:
        for d in range(1, groups):
            task = task_of[group_at(d)]
            base = task - lax.rem(task, 2)
            for i in range(2):
                act_staged[d, i] = act_mid[base + i]
            each = copy(act_staged.at[d], act_final.at[row, me], pick_send.at[d], pick_recv.at[d], "group", group_at(d))
            each.start()
            pick_copies.append(each)
        for i in range(2):
            act_final[row, me, i] = act_mid[start + i]
        for d in range(1, groups):
            arrived(act_final.at[row, back(d)], pick_send.at[d], pick_recv.at[d], "group", back(d))
    else:
        for i in range(2):
            act_final[row, 0, i] = act_mid[start + i]
    task_copies = [
        copy(act_final.at[row], act_final.at[row], task_send.at[d], task_recv.at[d], "dp", row_at(d))
        for d in range(1, dps)
    ]
    for each in task_copies:
        each.start()
    for d in range(1, groups):
        arrived(mid.at[back(d)], one_send.at[d], one_recv.at[d], "group", back(d))
    two_copies = []
    for d in range(1, groups):
        staged[d] = mid[owner[group_at(d)]]
        each = copy(staged.at[d], final.at[me], two_send.at[d], two_recv.at[d], "group", group_at(d))
        each.start()
        two_copies.append(each)
    final[me] = mid[owner[me]]

    for d in range(1, dps):
        arrived(cot_all.at[row_back(d)], cot_send.at[d], cot_recv.at[d], "dp", row_back(d))
    tokens = dps * acts.shape[0]
    cot_t = cot_all[...].reshape(tokens, order).T
    for d in range(1, dps):
        arrived(pairs.at[row_back(d), parity], own_send.at[d], own_recv.at[d], "dp", row_back(d))
        arrived(pairs.at[row_back(d), 1 - parity], other_send.at[d], other_recv.at[d], "dp", row_back(d))

    def gradient_of(halves):
        for i in range(2):
            part = dot(cot_t, halves[i].reshape(tokens, half))
            block_ref[:, i * half : (i + 1) * half] = part.astype(bf16)
        return block_ref[...]

    def gram(block, side):
        return jnp.where(side == 1, dot(block, block, ((0,), (0,))), dot(block, block, ((1,), (1,))))

    def unpacked(packed):
        found = {b: packed[at * tile : (at + 1) * tile] for at, b in enumerate(blocks)}
        count = range(order // tile)
        rows = [[found[i, j] if (i, j) in found else found[j, i].T for j in count] for i in count]
        return jnp.concatenate([jnp.concatenate(each, 1) for each in rows], 0)

    own = gradient_of([pairs[:, i] for i in range(2)])
    own_gram = gram(own, parity)
    arrived(root_in, root_send.at[0], root_recv.at[0], "group", partner)
    root_pair[1 - parity] = unpacked(root_in[...].astype(f32)).astype(bf16)
    left_part = dot(root_pair[0], own).astype(bf16)
    right = root_pair[1, :, pl.ds(pl.multiple_of(parity * half, half), half)]
    update[...] = dot(left_part, right).astype(bf16)

    for d in range(1, dps):
        arrived(act_final.at[row_back(d)], task_send.at[d], task_recv.at[d], "dp", row_back(d))
    task_block = gradient_of([act_final[:, :, i] for i in range(2)])
    new_stats[...] = decay_rate * stats[...] + gram(task_block, lax.rem(mine, 2))

    for d in range(1, groups):
        arrived(final.at[back(d)], two_send.at[d], two_recv.at[d], "group", back(d))
    whole = unpacked(final[...].reshape(lows.shape).astype(f32))
    shape = (order, order)
    eye = lax.broadcasted_iota(jnp.int32, shape, 0) == lax.broadcasted_iota(jnp.int32, shape, 1)
    identity = jnp.where(eye, 1.0, 0.0).astype(f32)
    matrix = decay_rate * whole + own_gram + ridge * identity
    new_roots[...] = newton_root(matrix, counts[me], identity).astype(bf16)
    sent = [near_copy, root_copy, *act_copies, *own_copies, *other_copies, *pick_copies]
    for each in [*sent, *task_copies, *cot_copies, *one_copies, *two_copies]:
        each.wait_send()


def per_device(acts, cotan, stats, roots, owner, task_of, counts):
    groups, dps = lax.axis_size("group"), lax.axis_size("dp")
    order, half = stats.shape[-1], acts.shape[1]
    count = range(order // tile)
    blocks = [(i, j) for i in count for j in count if j >= i]
    if len(blocks) * tile % (16 * groups):
        blocks = [(i, j) for i in count for j in count]
    rows = len(blocks) * tile
    cut = groups if acts.shape[0] % (16 * groups) == 0 else 1
    depth = acts.shape[0] // cut
    strips = pltpu.VMEM((groups, rows // groups, tile), bf16)
    in_vmem, in_smem = (pl.BlockSpec(memory_space=m) for m in (pltpu.VMEM, pltpu.SMEM))
    over_group, over_dp = (pltpu.SemaphoreType.DMA((n,)) for n in (groups, dps))
    update, new_stats, new_roots = pl.pallas_call(
        functools.partial(kernel, groups, dps, blocks),
        out_shape=(
            jax.ShapeDtypeStruct((order, half), bf16),
            jax.ShapeDtypeStruct((order, order), f32),
            jax.ShapeDtypeStruct((order, order), bf16),
        ),
        in_specs=[in_smem] * 3 + [pl.BlockSpec(memory_space=pltpu.HBM)] * 4,
        out_specs=(in_vmem,) * 3,
        scratch_shapes=[
            pltpu.VMEM((groups, depth, half), bf16),
            pltpu.VMEM((cut, 2, depth, half), bf16),
            pltpu.VMEM((dps, cut, 2, depth, half), bf16),
            pltpu.VMEM((dps, 2, *acts.shape), bf16),
            pltpu.VMEM((dps, acts.shape[0], order), bf16),
            pltpu.VMEM((rows, tile), bf16),
            strips,
            strips,
            strips,
            pltpu.VMEM((rows, tile), bf16),
            pltpu.VMEM((rows, tile), bf16),
            pltpu.VMEM((2, order, order), bf16),
            pltpu.VMEM((order, order), bf16),
            pltpu.VMEM((order, order), f32),
            *[over_group] * 8,
            *[over_dp] * 8,
            *[pltpu.SemaphoreType.DMA((1,))] * 4,
            pltpu.SemaphoreType.DMA((4,)),
        ],
        compiler_params=pltpu.CompilerParams(
            collective_id=0, has_side_effects=True, vmem_limit_bytes=54 * 2**20
        ),
    )(owner, task_of, counts, acts, cotan, stats[0, 0], roots[0, 0])
    return update, new_stats[None, None], new_roots[None, None]


def solution(mesh):
    return jax.shard_map(
        per_device,
        mesh=mesh,
        in_specs=(
            P("dp", "group"),
            P("dp", None),
            P("dp", "group", None, None),
            P("dp", "group", None, None),
            P(),
            P(),
            P(),
        ),
        out_specs=(P("dp", "group"), P("dp", "group", None, None), P("dp", "group", None, None)),
        check_vma=False,
    )
```

```python
import functools

import jax
import jax.numpy as jnp
from jax import lax
from jax.experimental import pallas as pl
from jax.experimental.pallas import tpu as pltpu
from jax.sharding import PartitionSpec as P

decay_rate = 0.9
ridge = 0.001
tile = 128
f32 = jnp.float32
bf16 = jnp.bfloat16


def dot(a, b, over=((1,), (0,))):
    return lax.dot_general(a, b, (over, ((), ())), preferred_element_type=f32)


def newton_root(matrix, turns, identity):
    size = jnp.sqrt(jnp.sum(matrix * matrix, keepdims=True))
    scaled = matrix * (1.0 / size)
    first = 1.25 * identity - 0.25 * scaled
    low = scaled.astype(bf16)
    square = dot(low, low)
    rest = ((square - 10.0 * scaled) * 0.0625).astype(bf16)
    product = 1.25 * scaled - 0.25 * square
    for _ in range(2):
        product = 1.5625 * product + dot(rest, product.astype(bf16))
    second = 1.25 * first - 0.25 * product
    return jnp.where(turns == 1, first, second) * (1.0 / jnp.sqrt(jnp.sqrt(size)))


def kernel(
    groups, dps, blocks,
    owner, task_of, counts, acts, cotan, stats_in, roots,
    update, new_stats, new_roots,
    act_mid, act_staged, act_final, pairs, cot_all, lows, mid, staged, final, root_low, root_in, root_pair, block_ref, stats, cot_turned,
    acts_send, acts_recv, pick_send, pick_recv, one_send, one_recv, two_send, two_recv,
    own_send, own_recv, other_send, other_recv, task_send, task_recv, cot_send, cot_recv,
    near_send, near_recv, root_send, root_recv, load_sem,
):
    me = lax.axis_index("group")
    row = lax.axis_index("dp")
    order = stats.shape[-1]
    half = acts.shape[1]
    parity = lax.rem(me, 2)
    partner = me + 1 - 2 * parity
    first = me - parity

    def group_at(d):
        return lax.rem(me + d, groups)

    def row_at(d):
        return lax.rem(row + d, dps)

    def copy(src, dst, send, recv, axis, to):
        return pltpu.make_async_remote_copy(
            src_ref=src, dst_ref=dst, send_sem=send, recv_sem=recv,
            device_id={axis: to}, device_id_type=pl.DeviceIdType.MESH,
        )

    barrier = pltpu.get_barrier_semaphore()
    for d in range(1, groups):
        pl.semaphore_signal(barrier, inc=1, device_id={"group": group_at(d)}, device_id_type=pl.DeviceIdType.MESH)
    for d in range(1, dps):
        pl.semaphore_signal(barrier, inc=1, device_id={"dp": row_at(d)}, device_id_type=pl.DeviceIdType.MESH)
    columns = cotan.at[:, pl.ds(pl.multiple_of(row * order, order), order)]
    stats_load, roots_load, acts_load, cotan_load = loads = [
        pltpu.make_async_copy(src, dst, load_sem.at[i])
        for i, (src, dst) in enumerate(
            [
                (stats_in, stats),
                (roots, root_pair.at[parity]),
                (acts, pairs.at[row, parity]),
                (columns, cot_all.at[row]),
            ]
        )
    ]
    for each in loads:
        each.start()
    strip = lows.shape[0] // groups
    pl.semaphore_wait(barrier, groups + dps - 2)

    def strip_of(g):
        return lows.at[pl.ds(pl.multiple_of(g * strip, strip), strip), :]

    cut = act_final.shape[1]
    depth = act_final.shape[3]

    def act_strip(g):
        return pl.ds(pl.multiple_of(g * depth, depth), depth) if cut > 1 else slice(None)

    act_copies = [
        copy(acts.at[act_strip(group_at(d)), :], act_mid.at[me], acts_send.at[d], acts_recv.at[d], "group", group_at(d))
        for d in range(1, groups)
    ]
    near_copy = copy(acts, pairs.at[row, parity], near_send.at[0], near_recv.at[0], "group", partner)
    own_copies = [
        copy(acts, pairs.at[row, parity], own_send.at[d], own_recv.at[d], "dp", row_at(d))
        for d in range(1, dps)
    ]
    cot_copies = []
    for d in range(1, dps):
        to = row_at(d)
        columns = cotan.at[:, pl.ds(pl.multiple_of(to * order, order), order)]
        cot_copies.append(copy(columns, cot_all.at[row], cot_send.at[d], cot_recv.at[d], "dp", to))
    one_copies = [
        copy(strip_of(group_at(d)), mid.at[me], one_send.at[d], one_recv.at[d], "group", group_at(d))
        for d in range(1, groups)
    ]
    root_copy = copy(root_low, root_in, root_send.at[0], root_recv.at[0], "group", partner)
    for each in [near_copy, *act_copies, *cot_copies, *own_copies]:
        each.start()
    stats_load.wait()
    for at, (i, j) in enumerate(blocks):
        part = stats[i * tile : (i + 1) * tile, j * tile : (j + 1) * tile].astype(bf16)
        lows[at * tile : (at + 1) * tile, :] = part
    for each in one_copies:
        each.start()
    mid[me] = lows[pl.ds(pl.multiple_of(me * strip, strip), strip), :]
    roots_load.wait()
    for at, (i, j) in enumerate(blocks):
        part = root_pair[parity, i * tile : (i + 1) * tile, j * tile : (j + 1) * tile]
        root_low[at * tile : (at + 1) * tile, :] = part
    root_copy.start()
    acts_load.wait()
    act_mid[me] = pairs[row, parity, act_strip(me), :]
    cotan_load.wait()
    mine = task_of[me]

    def back(d):
        return lax.rem(me + groups - d, groups)

    def row_back(d):
        return lax.rem(row + dps - d, dps)

    def arrived(place, send, recv, axis, source):
        copy(place, place, send, recv, axis, source).wait_recv()

    other = pairs.at[row, 1 - parity]
    arrived(other, near_send.at[0], near_recv.at[0], "group", partner)
    other_copies = [
        copy(other, other, other_send.at[d], other_recv.at[d], "dp", row_at(d)) for d in range(1, dps)
    ]
    for each in other_copies:
        each.start()

    for d in range(1, groups):
        arrived(act_mid.at[back(d)], acts_send.at[d], acts_recv.at[d], "group", back(d))
    start = mine - lax.rem(mine, 2)
    pick_copies = []
    if cut > 1:
        for d in range(1, groups):
            task = task_of[group_at(d)]
            base = task - lax.rem(task, 2)
            for i in range(2):
                act_staged[d, i] = act_mid[base + i]
            each = copy(act_staged.at[d], act_final.at[row, me], pick_send.at[d], pick_recv.at[d], "group", group_at(d))
            each.start()
            pick_copies.append(each)
        for i in range(2):
            act_final[row, me, i] = act_mid[start + i]
        for d in range(1, groups):
            arrived(act_final.at[row, back(d)], pick_send.at[d], pick_recv.at[d], "group", back(d))
    else:
        for i in range(2):
            act_final[row, 0, i] = act_mid[start + i]
    task_copies = [
        copy(act_final.at[row], act_final.at[row], task_send.at[d], task_recv.at[d], "dp", row_at(d))
        for d in range(1, dps)
    ]
    for each in task_copies:
        each.start()
    for d in range(1, dps):
        arrived(cot_all.at[row_back(d)], cot_send.at[d], cot_recv.at[d], "dp", row_back(d))
    tokens = dps * acts.shape[0]
    cot_turned[...] = cot_all[...].reshape(tokens, order).T
    for d in range(1, groups):
        arrived(mid.at[back(d)], one_send.at[d], one_recv.at[d], "group", back(d))
    two_copies = []
    for d in range(1, groups):
        staged[d] = mid[owner[group_at(d)]]
        each = copy(staged.at[d], final.at[me], two_send.at[d], two_recv.at[d], "group", group_at(d))
        each.start()
        two_copies.append(each)
    final[me] = mid[owner[me]]

    for d in range(1, dps):
        arrived(pairs.at[row_back(d), parity], own_send.at[d], own_recv.at[d], "dp", row_back(d))
        arrived(pairs.at[row_back(d), 1 - parity], other_send.at[d], other_recv.at[d], "dp", row_back(d))

    def gradient_of(halves):
        for i in range(2):
            part = dot(cot_turned[...], halves[i].reshape(tokens, half))
            block_ref[:, i * half : (i + 1) * half] = part.astype(bf16)
        return block_ref[...]

    def gram(block, side):
        return jnp.where(side == 1, dot(block, block, ((0,), (0,))), dot(block, block, ((1,), (1,))))

    def unpacked(packed):
        found = {b: packed[at * tile : (at + 1) * tile] for at, b in enumerate(blocks)}
        count = range(order // tile)
        rows = [[found[i, j] if (i, j) in found else found[j, i].T for j in count] for i in count]
        return jnp.concatenate([jnp.concatenate(each, 1) for each in rows], 0)

    own = gradient_of([pairs[:, i] for i in range(2)])
    own_gram = gram(own, parity)
    arrived(root_in, root_send.at[0], root_recv.at[0], "group", partner)
    root_pair[1 - parity] = unpacked(root_in[...].astype(f32)).astype(bf16)
    left_part = dot(root_pair[0], own).astype(bf16)
    right = root_pair[1, :, pl.ds(pl.multiple_of(parity * half, half), half)]
    update[...] = dot(left_part, right).astype(bf16)

    for d in range(1, dps):
        arrived(act_final.at[row_back(d)], task_send.at[d], task_recv.at[d], "dp", row_back(d))
    task_block = gradient_of([act_final[:, :, i] for i in range(2)])
    new_stats[...] = decay_rate * stats[...] + gram(task_block, lax.rem(mine, 2))

    for d in range(1, groups):
        arrived(final.at[back(d)], two_send.at[d], two_recv.at[d], "group", back(d))
    whole = unpacked(final[...].reshape(lows.shape).astype(f32))
    shape = (order, order)
    eye = lax.broadcasted_iota(jnp.int32, shape, 0) == lax.broadcasted_iota(jnp.int32, shape, 1)
    identity = jnp.where(eye, 1.0, 0.0).astype(f32)
    matrix = decay_rate * whole + own_gram + ridge * identity
    new_roots[...] = newton_root(matrix, counts[me], identity).astype(bf16)
    sent = [near_copy, root_copy, *act_copies, *own_copies, *other_copies, *pick_copies]
    for each in [*sent, *task_copies, *cot_copies, *one_copies, *two_copies]:
        each.wait_send()


def per_device(acts, cotan, stats, roots, owner, task_of, counts):
    groups, dps = lax.axis_size("group"), lax.axis_size("dp")
    order, half = stats.shape[-1], acts.shape[1]
    count = range(order // tile)
    blocks = [(i, j) for i in count for j in count if j >= i]
    if len(blocks) * tile % (16 * groups):
        blocks = [(i, j) for i in count for j in count]
    rows = len(blocks) * tile
    cut = groups if acts.shape[0] % (16 * groups) == 0 else 1
    depth = acts.shape[0] // cut
    strips = pltpu.VMEM((groups, rows // groups, tile), bf16)
    in_vmem, in_smem = (pl.BlockSpec(memory_space=m) for m in (pltpu.VMEM, pltpu.SMEM))
    over_group, over_dp = (pltpu.SemaphoreType.DMA((n,)) for n in (groups, dps))
    update, new_stats, new_roots = pl.pallas_call(
        functools.partial(kernel, groups, dps, blocks),
        out_shape=(
            jax.ShapeDtypeStruct((order, half), bf16),
            jax.ShapeDtypeStruct((order, order), f32),
            jax.ShapeDtypeStruct((order, order), bf16),
        ),
        in_specs=[in_smem] * 3 + [pl.BlockSpec(memory_space=pltpu.HBM)] * 4,
        out_specs=(in_vmem,) * 3,
        scratch_shapes=[
            pltpu.VMEM((groups, depth, half), bf16),
            pltpu.VMEM((cut, 2, depth, half), bf16),
            pltpu.VMEM((dps, cut, 2, depth, half), bf16),
            pltpu.VMEM((dps, 2, *acts.shape), bf16),
            pltpu.VMEM((dps, acts.shape[0], order), bf16),
            pltpu.VMEM((rows, tile), bf16),
            strips,
            strips,
            strips,
            pltpu.VMEM((rows, tile), bf16),
            pltpu.VMEM((rows, tile), bf16),
            pltpu.VMEM((2, order, order), bf16),
            pltpu.VMEM((order, order), bf16),
            pltpu.VMEM((order, order), f32),
            pltpu.VMEM((order, dps * acts.shape[0]), bf16),
            *[over_group] * 8,
            *[over_dp] * 8,
            *[pltpu.SemaphoreType.DMA((1,))] * 4,
            pltpu.SemaphoreType.DMA((4,)),
        ],
        compiler_params=pltpu.CompilerParams(
            collective_id=0, has_side_effects=True, vmem_limit_bytes=54 * 2**20
        ),
    )(owner, task_of, counts, acts, cotan, stats[0, 0], roots[0, 0])
    return update, new_stats[None, None], new_roots[None, None]


def solution(mesh):
    return jax.shard_map(
        per_device,
        mesh=mesh,
        in_specs=(
            P("dp", "group"),
            P("dp", None),
            P("dp", "group", None, None),
            P("dp", "group", None, None),
            P(),
            P(),
            P(),
        ),
        out_specs=(P("dp", "group"), P("dp", "group", None, None), P("dp", "group", None, None)),
        check_vma=False,
    )
```
